512 devices in a mesh: row: 32 (over z, x_hi), col: 16 (over x_lo, y, core).
Axes of the slice: x: 4 (x_hi: 2, x_lo: 2; x = x_hi * 2 + x_lo), y: 4, z: 16, core: 2. Of those that a mesh axis runs over, the one named last changes fastest.
Arguments:
- upper: float32 [1, 32, 6, 16, 128, 128], P(None, 'row', None, 'col'), may hold values from -1 to 1
- mask: int32 [1, 32, 6, 16], P(None, 'row', None, 'col'), may hold values from 0 to 1, as said below
Outputs:
- square: float32 [1, 32, 24, 16, 128, 128], P(None, 'row', None, 'col')
The draws below stay inside these ranges and needn't reach their ends.
Inputs may be any that keep to these rules, and one draw needn't show every extreme that they name: A stored block is present where mask is 1; blocks on the main diagonal are always present.
All inputs are finite; a program needn't handle non-finite values.
Results may differ from the reference program's by a relative error of at most 0.0003.
Values sent between devices are 32-bit elements; how exact they have to be, the bound alone decides.
No kernel may reach another device: no remote copies, remote signals or barrier semaphores. Data moves between devices by JAX's collectives and lax.ppermute only.
A program may use at most 64 MiB of HBM per device.

```python
import jax
import jax.numpy as jnp
from jax import lax

BS = 128
HB = 96
RB = 1
HQ = 6
N_ROW = 32
N_COL = 16


def draw_mask(key, part):
    key = jax.random.fold_in(key, 11)
    offset = jnp.arange(HQ, dtype=jnp.int32)[:, None] * N_COL + jnp.arange(N_COL, dtype=jnp.int32)[None, :]
    threshold = 1000 - 800 * offset // HB
    dice_roll = jax.random.randint(key, (RB, N_ROW, HQ, N_COL), 0, 1000, dtype=jnp.int32)
    return jnp.where(dice_roll < threshold[None, None], 1, 0).astype(jnp.int32)


def block_levels(stream_key, dims, shards, smallest, top_value):
    loudness = 1.0
    for axis_at, blocks in shards:
        draws = jax.random.uniform(jax.random.fold_in(jax.random.fold_in(stream_key, 6), axis_at), (blocks,), jnp.float32, smallest / len(shards), top_value / len(shards))
        loudness = loudness * jnp.repeat(jnp.exp(draws), dims[axis_at] // blocks).reshape((-1,) + (1,) * (len(dims) - 1 - axis_at))
    return loudness


def gaussian(own_key, dims, deviation, limit, shards=(), kind=jnp.bfloat16):
    array = jax.random.normal(own_key, dims, jnp.float32) * deviation
    if len(shards) > 0:
        array = block_levels(own_key, dims, shards, -0.22, 0.18) * array
    return jnp.clip(array, min=-limit, max=limit).astype(kind)


def setup_inputs(seed: int = 0) -> dict:
    arg_keys = jax.random.split(jax.random.key(seed), 3)
    upper = gaussian(arg_keys[0], (RB, N_ROW, HQ, N_COL, BS, BS), 0.16, 1.0, ((1, 32), (3, 16)), jnp.float32)
    mask = draw_mask(jax.random.fold_in(arg_keys[2], 71), 0)
    return dict(upper=upper, mask=mask)


def place_run(square_row, product_row, column_class, first_slot):
    run_width = product_row.shape[0]
    block_size = product_row.shape[1]
    zero_index = jnp.zeros((), jnp.int32)
    column_class = column_class.astype(jnp.int32)
    first_slot = first_slot.astype(jnp.int32)
    starts = (column_class, first_slot, zero_index, zero_index)
    current = lax.dynamic_slice(square_row, starts, (1, run_width, block_size, block_size))
    return lax.dynamic_update_slice(square_row, current + product_row[None], starts)


def roll_rows(column, amount):
    return jnp.roll(column, amount, axis=0)


def reference(upper, mask):
    local_rows = upper.shape[0]
    row_count = upper.shape[1]
    slot_count = upper.shape[2]
    col_count = upper.shape[3]
    block_size = upper.shape[4]
    block_rows = local_rows * row_count
    band_width = slot_count * col_count
    weights = mask.reshape(block_rows, band_width).astype(jnp.float32)
    stored = upper.reshape(block_rows, band_width, block_size, block_size) * weights[:, :, None, None]
    diagonal = stored[:, 0] + jnp.swapaxes(stored[:, 0], -1, -2)
    stored = stored.at[:, 0].set(diagonal)
    distance = jnp.arange(band_width, dtype=jnp.int32)
    mirrored = jax.vmap(roll_rows, in_axes=(1, 0), out_axes=1)(stored, distance)
    mirrored = jnp.swapaxes(mirrored, -1, -2)
    empty_row = jnp.zeros((block_rows, 1, block_size, block_size), jnp.float32)
    full_band = jnp.concatenate([empty_row, jnp.flip(mirrored[:, 1:], axis=1), stored], axis=1)
    row_ids = jnp.arange(block_rows, dtype=jnp.int32)
    slot_ids = jnp.arange(2 * slot_count, dtype=jnp.int32)
    square = jnp.zeros((block_rows, col_count, 4 * slot_count, block_size, block_size), jnp.float32)

    def one_offset(accumulated, position):
        inner_offset = position - band_width
        left_blocks = lax.dynamic_index_in_dim(full_band, position, 1, keepdims=False)
        neighbour_rows = ((row_ids + inner_offset) % block_rows).astype(jnp.int32)
        for step_number in range(2):
            residue = ((-row_ids - step_number) % col_count).astype(jnp.int32)
            pick_index = residue[:, None] + col_count * slot_ids[None, :]
            right_blocks = full_band[neighbour_rows[:, None], pick_index]
            product = jnp.einsum("rij,rmjk->rmik", left_blocks, right_blocks, precision=lax.Precision.HIGHEST, preferred_element_type=jnp.float32)
            total_shift = inner_offset + residue
            first_slot = (jnp.floor_divide(total_shift, col_count) + slot_count).astype(jnp.int32)
            column_class = ((row_ids + total_shift) % col_count).astype(jnp.int32)
            accumulated = jax.vmap(place_run)(accumulated, product, column_class, first_slot)
        return accumulated, None

    square, _ = lax.scan(one_offset, square, jnp.arange(2 * band_width, dtype=jnp.int32))
    square = square.reshape(local_rows, row_count, col_count, 4 * slot_count, block_size, block_size)
    return square.transpose(0, 1, 3, 2, 4, 5)
```

```python
import jax
import jax.numpy as jnp
from jax import lax
from jax.experimental import pallas as pl
from jax.experimental.pallas import tpu as pltpu
from jax.sharding import PartitionSpec as P

MESH_AXES = ("row", "col")


def permute(value, row_count, col_count, source_of):
    pairs = []
    for p in range(row_count):
        for q in range(col_count):
            source_row, source_col = source_of(p, q)
            source = source_row % row_count * col_count + source_col % col_count
            pairs.append((source, p * col_count + q))
    return lax.ppermute(value, MESH_AXES, pairs)


def split(value):
    high = value.astype(jnp.bfloat16)
    return high, (value - high.astype(jnp.float32)).astype(jnp.bfloat16)


def band_kernel(mirrored, scalars, mirror_a, mirror_b, stored, right_a, right_b, total, out, left_high, left_low, tiles_high, tiles_low):
    half = mirror_a.shape[0]
    size = stored.shape[1]
    slots = stored.shape[0]
    left_zero = scalars[0]
    flip = scalars[1]
    right_zero = scalars[2]
    first = scalars[3]

    def put_left(slot, block):
        high, low = split(block)
        at = (pl.ds(slot // 2 * size, size), pl.ds(slot % 2 * size, size))
        left_high[at] = high
        left_low[at] = low

    for pair in range(half):
        pick = jnp.minimum(half - 1 - pair + left_zero, half - 1)
        block = mirror_a[pick].T
        if pair == 0:
            block = block * (1 - left_zero).astype(jnp.float32)
        put_left(2 * pair, block)
        put_left(2 * pair + 1, mirror_b[half - 1 - pair].T)
    for slot in range(slots):
        block = stored[slot]
        if slot == 0:
            block = block + block.T * left_zero.astype(jnp.float32)
        put_left(slots + slot, block)

    def right_block(layer, slot):
        swapped = flip if layer == 0 else 1 - flip
        if mirrored:
            stored_slot = slots - 1 - slot
            swapped = swapped if stored_slot % 2 == 0 else 1 - swapped
            both = jnp.where(swapped == 0, right_a[stored_slot], right_b[stored_slot])
            if stored_slot == 0:
                both = both * (1 - right_zero).astype(jnp.float32)
            return both.T
        both = jnp.where(swapped == 0, right_a[slot], right_b[slot])
        if slot == 0:
            both = both + both.T * right_zero.astype(jnp.float32)
        return both

    zero = jnp.zeros((size, size), jnp.bfloat16)
    tile_count = slots // 2 + 1
    for tile in range(tile_count):
        for layer in range(2):
            for column in range(2):
                slot = 2 * tile + column - layer
                at = (tile, pl.ds(layer * size, size), pl.ds(column * size, size))
                if 0 <= slot < slots:
                    high, low = split(right_block(layer, slot))
                    tiles_high[at] = high
                    tiles_low[at] = low
                else:
                    tiles_high[at] = zero
                    tiles_low[at] = zero

    out[...] = total[...]
    left_pairs = left_high.shape[0] // size
    for tile in range(tile_count):
        high = tiles_high[tile]
        low = tiles_low[tile]
        for pair in range(left_pairs):
            rows = pl.ds(pair * size, size)
            part_high = left_high[rows, :]
            part = jnp.dot(part_high, high, preferred_element_type=jnp.float32)
            part = part + jnp.dot(part_high, low, preferred_element_type=jnp.float32)
            part = part + jnp.dot(left_low[rows, :], high, preferred_element_type=jnp.float32)
            at = 2 * (tile + pair) + first
            out[at] += part[:, :size]
            if tile < tile_count - 1:
                out[at + 1] += part[:, size:]


def add_products(total, mirrored, scalars, mirror_a, mirror_b, stored, right_a, right_b):
    slots, size, _ = stored.shape
    vmem = pl.BlockSpec(memory_space=pltpu.VMEM)

    def kernel(*refs):
        band_kernel(mirrored, *refs)

    return pl.pallas_call(
        kernel,
        out_shape=jax.ShapeDtypeStruct(total.shape, jnp.float32),
        in_specs=[pl.BlockSpec(memory_space=pltpu.SMEM)] + [vmem] * 6,
        out_specs=vmem,
        scratch_shapes=[
            pltpu.VMEM((slots * size, 2 * size), jnp.bfloat16),
            pltpu.VMEM((slots * size, 2 * size), jnp.bfloat16),
            pltpu.VMEM((slots // 2 + 1, 2 * size, 2 * size), jnp.bfloat16),
            pltpu.VMEM((slots // 2 + 1, 2 * size, 2 * size), jnp.bfloat16),
        ],
        compiler_params=pltpu.CompilerParams(vmem_limit_bytes=24 * 1024 * 1024),
        cost_estimate=pl.CostEstimate(flops=4 * slots * slots * size**3 * 3, bytes_accessed=4 * 1024 * 1024, transcendentals=0),
    )(scalars, mirror_a, mirror_b, stored, right_a, right_b, total)


def per_device(upper, mask):
    row_count = lax.axis_size("row")
    col_count = lax.axis_size("col")
    p = lax.axis_index("row")
    q = lax.axis_index("col")
    slots = upper.shape[2]
    size = upper.shape[4]
    b = p % col_count

    def send(value, source_of):
        return permute(value, row_count, col_count, source_of)

    present = mask.reshape(slots).astype(jnp.float32)
    stored = upper.reshape(slots, size, size) * present[:, None, None]

    by_parity = stored.reshape(slots // 2, 2, size, size)
    even, odd = by_parity[:, 0], by_parity[:, 1]
    at_zero = q == 0
    for_left = jnp.concatenate([jnp.where(at_zero, even, odd), jnp.where(at_zero, odd, even)])
    via_left = send(for_left, lambda p, q: (p, q - 2 * p))
    via_upper = send(stored, lambda p, q: (p, p - q))
    via_lower = send(stored, lambda p, q: (p, q - p))
    stored_next = send(stored, lambda p, q: (p, q + 1))

    mirror = []
    upper_right = []
    lower_right = []
    for layer in range(2):
        shift = layer * col_count

        def from_sum(p, q):
            return (p + q + shift, 2 * p + q)

        half = via_left[layer * (slots // 2) : (layer + 1) * (slots // 2)]
        mirror.append(send(half, from_sum))
        upper_right.append(send(via_upper, from_sum))
    for layer in range(2):
        shift = layer * col_count

        def from_col(p, q):
            return (q + p // col_count * col_count + shift, p + q)

        lower_right.append(send(via_lower, from_col))

    def up_one(value):
        return send(value, lambda p, q: (p + 1, q))

    def along_one(value):
        return send(value, lambda p, q: (p, q + 1))

    mirror_next = [along_one(value) for value in mirror]
    upper_next = [up_one(value) for value in upper_right]
    lower_next = [up_one(value) for value in lower_right]

    def scalars(step, mirrored):
        start = (q + step) % col_count
        right = (-b - step) % col_count
        target = (q - b) % col_count
        carry = (start + right - target) // col_count
        left_zero = (start == 0).astype(jnp.int32)
        right_zero = (right == 0).astype(jnp.int32)
        flip = (q + step >= col_count).astype(jnp.int32)
        first = carry + (right_zero if mirrored else slots)
        return jnp.stack([left_zero, flip, right_zero, first]).astype(jnp.int32)

    total = jnp.zeros((4 * slots, size, size), jnp.float32)
    total = add_products(total, False, scalars(0, False), *mirror, stored, *upper_right)
    total = add_products(total, False, scalars(1, False), *mirror_next, stored_next, *upper_next)
    total = add_products(total, True, scalars(0, True), *mirror, stored, *lower_right)
    total = add_products(total, True, scalars(1, True), *mirror_next, stored_next, *lower_next)
    return total.reshape(1, 1, 4 * slots, 1, size, size)


def solution(mesh):
    in_specs = (P(None, "row", None, "col", None, None), P(None, "row", None, "col"))
    out_specs = P(None, "row", None, "col", None, None)
    return jax.shard_map(
        per_device, mesh=mesh, in_specs=in_specs, out_specs=out_specs, check_vma=False
    )
```

```python
import jax
import jax.numpy as jnp
from jax import lax
from jax.experimental import pallas as pl
from jax.experimental.pallas import tpu as pltpu
from jax.sharding import PartitionSpec as P

MESH_AXES = ("row", "col")


def permute(value, row_count, col_count, source_of):
    pairs = []
    for p in range(row_count):
        for q in range(col_count):
            source_row, source_col = source_of(p, q)
            source = source_row % row_count * col_count + source_col % col_count
            pairs.append((source, p * col_count + q))
    return lax.ppermute(value, MESH_AXES, pairs)


def split(value):
    high = value.astype(jnp.bfloat16)
    return high, (value - high.astype(jnp.float32)).astype(jnp.bfloat16)


def band_kernel(mirrored, scalars, mirror_a, mirror_b, stored, right_a, right_b, total, out, left_high, left_low, tiles_high, tiles_low):
    half = mirror_a.shape[0]
    size = stored.shape[1]
    slots = stored.shape[0]
    left_zero = scalars[0]
    flip = scalars[1]
    right_zero = scalars[2]
    first = scalars[3]
    left_swap = scalars[4]
    right_swap = scalars[5]

    def put_left(slot, block):
        high, low = split(block)
        at = (pl.ds(slot // 2 * size, size), pl.ds(slot % 2 * size, size))
        left_high[at] = high
        left_low[at] = low

    for pair in range(half):
        pick = jnp.minimum(half - 1 - pair + left_zero, half - 1)
        block = jnp.where(left_swap == 0, mirror_a[pick], mirror_b[pick]).T
        if pair == 0:
            block = block * (1 - left_zero).astype(jnp.float32)
        put_left(2 * pair, block)
        put_left(2 * pair + 1, jnp.where(left_swap == 0, mirror_b[half - 1 - pair], mirror_a[half - 1 - pair]).T)
    for slot in range(slots):
        block = stored[slot]
        if slot == 0:
            block = block + block.T * left_zero.astype(jnp.float32)
        put_left(slots + slot, block)

    def right_block(layer, slot):
        swapped = (flip + right_swap + layer) % 2
        if mirrored:
            stored_slot = slots - 1 - slot
            swapped = swapped if stored_slot % 2 == 0 else 1 - swapped
            both = jnp.where(swapped == 0, right_a[stored_slot], right_b[stored_slot])
            if stored_slot == 0:
                both = both * (1 - right_zero).astype(jnp.float32)
            return both.T
        both = jnp.where(swapped == 0, right_a[slot], right_b[slot])
        if slot == 0:
            both = both + both.T * right_zero.astype(jnp.float32)
        return both

    zero = jnp.zeros((size, size), jnp.bfloat16)
    tile_count = slots // 2 + 1
    for tile in range(tile_count):
        for layer in range(2):
            for column in range(2):
                slot = 2 * tile + column - layer
                at = (tile, pl.ds(layer * size, size), pl.ds(column * size, size))
                if 0 <= slot < slots:
                    high, low = split(right_block(layer, slot))
                    tiles_high[at] = high
                    tiles_low[at] = low
                else:
                    tiles_high[at] = zero
                    tiles_low[at] = zero

    out[...] = total[...]
    left_pairs = left_high.shape[0] // size
    for tile in range(tile_count):
        high = tiles_high[tile]
        low = tiles_low[tile]
        for pair in range(left_pairs):
            rows = pl.ds(pair * size, size)
            part_high = left_high[rows, :]
            part = jnp.dot(part_high, high, preferred_element_type=jnp.float32)
            part = part + jnp.dot(part_high, low, preferred_element_type=jnp.float32)
            part = part + jnp.dot(left_low[rows, :], high, preferred_element_type=jnp.float32)
            at = 2 * (tile + pair) + first
            out[at] += part[:, :size]
            if tile < tile_count - 1:
                out[at + 1] += part[:, size:]


def add_products(total, mirrored, scalars, mirror_a, mirror_b, stored, right_a, right_b):
    slots, size, _ = stored.shape
    vmem = pl.BlockSpec(memory_space=pltpu.VMEM)

    def kernel(*refs):
        band_kernel(mirrored, *refs)

    return pl.pallas_call(
        kernel,
        out_shape=jax.ShapeDtypeStruct(total.shape, jnp.float32),
        in_specs=[pl.BlockSpec(memory_space=pltpu.SMEM)] + [vmem] * 6,
        out_specs=vmem,
        scratch_shapes=[
            pltpu.VMEM((slots * size, 2 * size), jnp.bfloat16),
            pltpu.VMEM((slots * size, 2 * size), jnp.bfloat16),
            pltpu.VMEM((slots // 2 + 1, 2 * size, 2 * size), jnp.bfloat16),
            pltpu.VMEM((slots // 2 + 1, 2 * size, 2 * size), jnp.bfloat16),
        ],
        compiler_params=pltpu.CompilerParams(vmem_limit_bytes=24 * 1024 * 1024),
        cost_estimate=pl.CostEstimate(flops=4 * slots * slots * size**3 * 3, bytes_accessed=4 * 1024 * 1024, transcendentals=0),
    )(scalars, mirror_a, mirror_b, stored, right_a, right_b, total)


def per_device(upper, mask):
    row_count = lax.axis_size("row")
    col_count = lax.axis_size("col")
    p = lax.axis_index("row")
    q = lax.axis_index("col")
    slots = upper.shape[2]
    size = upper.shape[4]
    half = slots // 2
    middle = col_count // 2

    def send(value, source_of):
        return permute(value, row_count, col_count, source_of)

    def after(value, *earlier):
        return lax.optimization_barrier((value, *earlier))[0]

    def shift_of(amount, order):
        near_is_same = amount < middle
        return amount if near_is_same == (order == 0) else amount + col_count

    def row_from(p, q):
        return p - q if (p + q) % 2 == 0 else p + q

    def signed(p, value):
        return value if p % 2 == 0 else -value

    def from_line(p, line, order):
        amount = shift_of(line, order)
        return (p + signed(p, amount), line)

    def sum_source(order):
        return lambda p, q: from_line(p, signed(p, q) % col_count, order)

    def col_source(order):
        return lambda p, q: from_line(p, signed(p, q - p) % col_count, order)

    present = mask.reshape(slots).astype(jnp.float32)
    stored = upper.reshape(slots, size, size) * present[:, None, None]
    by_parity = stored.reshape(half, 2, size, size)
    even, odd = by_parity[:, 0], by_parity[:, 1]
    target = -q % col_count
    near_is_other = jnp.where((p + target) % 2 == 0, target >= middle, target > middle)
    odd_first = (q != 0) != near_is_other
    for_left = jnp.concatenate([jnp.where(odd_first, odd, even), jnp.where(odd_first, even, odd)])

    via_upper = send(stored, lambda p, q: (p, -row_from(p, q)))
    via_left = send(for_left, lambda p, q: (p, row_from(p, q) - p))
    via_lower = send(after(stored, via_upper, via_left), lambda p, q: (p, row_from(p, q) + 1))
    first = [None, None]
    second = [None, None]
    for order in (0, 1):
        half_of_left = via_left[order * half : (order + 1) * half]
        first[order] = send(jnp.concatenate([via_upper, half_of_left]), sum_source(order))
    for order in (0, 1):
        second[order] = send(via_lower, col_source(order))
    u_near = send(first[0][:slots], lambda p, q: (p + 1, q))
    d_near = send(second[0], lambda p, q: (p - 1, q))
    first[1] = after(first[1], u_near)
    upper_next = [u_near, send(first[1][:slots], lambda p, q: (p + 1, q))]
    second[1] = after(second[1], d_near)
    lower_right = [d_near, send(second[1], lambda p, q: (p - 1, q))]
    upper_right = [value[:slots] for value in first]
    mirror = [value[slots:] for value in first]
    lower_next = second
    moved = send(jnp.concatenate(mirror), lambda p, q: (p, q + 1))
    mirror_next = [moved[:half], moved[half:]]
    stored_next = send(after(stored, first[0], second[0]), lambda p, q: (p, q + 1))

    def scalars(step):
        row = (p + step) % row_count
        start = (q + step) % col_count
        right = -row % col_count
        carry = (start + right - (q - p) % col_count) // col_count
        left_zero = start == 0
        right_zero = right == 0
        flip = q + step >= col_count
        left_swap = jnp.where(p % 2 == 0, start >= middle, start > middle)
        upper_swap = jnp.where(row % 2 == 0, q >= middle, q > middle)
        landed = (row - 1) % row_count
        sign = 1 - 2 * (landed % 2)
        amount = sign * (q - landed) % col_count
        near = landed + sign * amount + jnp.where(amount < middle, 0, col_count)
        lower_swap = ((near - q) % row_count // col_count + row // col_count) % 2
        return left_zero, flip, right_zero, carry, left_swap, upper_swap, lower_swap

    def packed(*values):
        return jnp.stack([jnp.asarray(value, jnp.int32) for value in values])

    def right_scalars(step, mirrored):
        left_zero, flip, right_zero, carry, left_swap, upper_swap, lower_swap = scalars(step)
        if mirrored:
            return packed(left_zero, flip, right_zero, carry + right_zero, left_swap, lower_swap)
        return packed(left_zero, flip, right_zero, carry + slots, left_swap, upper_swap)

    total = jnp.zeros((4 * slots, size, size), jnp.float32)
    total = add_products(total, False, right_scalars(0, False), *mirror, stored, *upper_right)
    total = add_products(total, True, right_scalars(1, True), *mirror_next, stored_next, *lower_next)
    total = add_products(total, False, right_scalars(1, False), *mirror_next, stored_next, *upper_next)
    total = add_products(total, True, right_scalars(0, True), *mirror, stored, *lower_right)
    return total.reshape(1, 1, 4 * slots, 1, size, size)


def solution(mesh):
    in_specs = (P(None, "row", None, "col", None, None), P(None, "row", None, "col"))
    out_specs = P(None, "row", None, "col", None, None)
    return jax.shard_map(
        per_device, mesh=mesh, in_specs=in_specs, out_specs=out_specs, check_vma=False
    )
```

```python
import jax
import jax.numpy as jnp
from jax import lax
from jax.experimental import pallas as pl
from jax.experimental.pallas import tpu as pltpu
from jax.sharding import PartitionSpec as P

MESH_AXES = ("row", "col")


def permute(value, row_count, col_count, source_of):
    pairs = []
    for p in range(row_count):
        for q in range(col_count):
            source_row, source_col = source_of(p, q)
            source = source_row % row_count * col_count + source_col % col_count
            pairs.append((source, p * col_count + q))
    return lax.ppermute(value, MESH_AXES, pairs)


def split(value):
    high = value.astype(jnp.bfloat16)
    return high, (value - high.astype(jnp.float32)).astype(jnp.bfloat16)


def band_kernel(mirrored, scalars, mirror_a, mirror_b, stored, right_a, right_b, total, out, left_high, left_low, tiles_high, tiles_low):
    half = mirror_a.shape[0]
    size = stored.shape[1]
    slots = stored.shape[0]
    left_zero = scalars[0]
    flip = scalars[1]
    right_zero = scalars[2]
    first = scalars[3]
    left_swap = scalars[4]
    right_swap = scalars[5]

    def put_left(slot, block):
        high, low = split(block)
        at = (pl.ds(slot // 2 * size, size), pl.ds(slot % 2 * size, size))
        left_high[at] = high
        left_low[at] = low

    for pair in range(half):
        pick = jnp.minimum(half - 1 - pair + left_zero, half - 1)
        block = jnp.where(left_swap == 0, mirror_a[pick], mirror_b[pick]).T
        if pair == 0:
            block = block * (1 - left_zero).astype(jnp.float32)
        put_left(2 * pair, block)
        put_left(2 * pair + 1, jnp.where(left_swap == 0, mirror_b[half - 1 - pair], mirror_a[half - 1 - pair]).T)
    for slot in range(slots):
        block = stored[slot]
        if slot == 0:
            block = block + block.T * left_zero.astype(jnp.float32)
        put_left(slots + slot, block)

    def right_block(layer, slot):
        swapped = (flip + right_swap + layer) % 2
        if mirrored:
            stored_slot = slots - 1 - slot
            swapped = swapped if stored_slot % 2 == 0 else 1 - swapped
            both = jnp.where(swapped == 0, right_a[stored_slot], right_b[stored_slot])
            if stored_slot == 0:
                both = both * (1 - right_zero).astype(jnp.float32)
            return both.T
        both = jnp.where(swapped == 0, right_a[slot], right_b[slot])
        if slot == 0:
            both = both + both.T * right_zero.astype(jnp.float32)
        return both

    zero = jnp.zeros((size, size), jnp.bfloat16)
    tile_count = slots // 2 + 1
    for tile in range(tile_count):
        for layer in range(2):
            for column in range(2):
                slot = 2 * tile + column - layer
                at = (tile, pl.ds(layer * size, size), pl.ds(column * size, size))
                if 0 <= slot < slots:
                    high, low = split(right_block(layer, slot))
                    tiles_high[at] = high
                    tiles_low[at] = low
                else:
                    tiles_high[at] = zero
                    tiles_low[at] = zero

    out[...] = total[...]
    left_pairs = left_high.shape[0] // size
    for tile in range(tile_count):
        high = tiles_high[tile]
        low = tiles_low[tile]
        for pair in range(left_pairs):
            rows = pl.ds(pair * size, size)
            part_high = left_high[rows, :]
            part = jnp.dot(part_high, high, preferred_element_type=jnp.float32)
            part = part + jnp.dot(part_high, low, preferred_element_type=jnp.float32)
            part = part + jnp.dot(left_low[rows, :], high, preferred_element_type=jnp.float32)
            at = 2 * (tile + pair) + first
            out[at] += part[:, :size]
            if tile < tile_count - 1:
                out[at + 1] += part[:, size:]


def add_products(total, mirrored, scalars, mirror_a, mirror_b, stored, right_a, right_b):
    slots, size, _ = stored.shape
    vmem = pl.BlockSpec(memory_space=pltpu.VMEM)

    def kernel(*refs):
        band_kernel(mirrored, *refs)

    return pl.pallas_call(
        kernel,
        out_shape=jax.ShapeDtypeStruct(total.shape, jnp.float32),
        in_specs=[pl.BlockSpec(memory_space=pltpu.SMEM)] + [vmem] * 6,
        out_specs=vmem,
        scratch_shapes=[
            pltpu.VMEM((slots * size, 2 * size), jnp.bfloat16),
            pltpu.VMEM((slots * size, 2 * size), jnp.bfloat16),
            pltpu.VMEM((slots // 2 + 1, 2 * size, 2 * size), jnp.bfloat16),
            pltpu.VMEM((slots // 2 + 1, 2 * size, 2 * size), jnp.bfloat16),
        ],
        compiler_params=pltpu.CompilerParams(vmem_limit_bytes=24 * 1024 * 1024),
        cost_estimate=pl.CostEstimate(flops=4 * slots * slots * size**3 * 3, bytes_accessed=4 * 1024 * 1024, transcendentals=0),
    )(scalars, mirror_a, mirror_b, stored, right_a, right_b, total)


def per_device(upper, mask):
    row_count = lax.axis_size("row")
    col_count = lax.axis_size("col")
    p = lax.axis_index("row")
    q = lax.axis_index("col")
    slots = upper.shape[2]
    size = upper.shape[4]
    half = slots // 2
    middle = col_count // 2

    def send(value, source_of):
        return permute(value, row_count, col_count, source_of)

    def after(value, *earlier):
        return lax.optimization_barrier((value, *earlier))[0]

    def shift_of(amount, order):
        near_is_same = amount < middle
        return amount if near_is_same == (order == 0) else amount + col_count

    def row_from(p, q):
        return p - q if (p + q) % 2 == 0 else p + q

    def signed(p, value):
        return value if p % 2 == 0 else -value

    def from_line(p, line, order):
        amount = shift_of(line, order)
        return (p + signed(p, amount), line)

    def sum_source(order):
        return lambda p, q: from_line(p, signed(p, q) % col_count, order)

    def col_source(order):
        return lambda p, q: from_line(p, signed(p, q - p) % col_count, order)

    present = mask.reshape(slots).astype(jnp.float32)
    stored = upper.reshape(slots, size, size) * present[:, None, None]
    by_parity = stored.reshape(half, 2, size, size)
    even, odd = by_parity[:, 0], by_parity[:, 1]
    target = -q % col_count
    near_is_other = jnp.where((p + target) % 2 == 0, target >= middle, target > middle)
    odd_first = (q != 0) != near_is_other
    for_left = jnp.concatenate([jnp.where(odd_first, odd, even), jnp.where(odd_first, even, odd)])

    via_upper = send(stored, lambda p, q: (p, -row_from(p, q)))
    via_left = send(for_left, lambda p, q: (p, row_from(p, q) - p))
    via_lower = send(after(stored, via_upper, via_left), lambda p, q: (p, row_from(p, q) + 1))
    first = [None, None]
    second = [None, None]
    for order in (0, 1):
        half_of_left = via_left[order * half : (order + 1) * half]
        first[order] = send(jnp.concatenate([via_upper, half_of_left]), sum_source(order))
    for order in (0, 1):
        second[order] = send(via_lower, col_source(order))
    upper_next = [None, None]
    lower_right = [None, None]
    upper_next[1] = send(first[1][:slots], lambda p, q: (p + 1, q))
    lower_right[0] = send(second[0], lambda p, q: (p - 1, q))
    first[0] = after(first[0], upper_next[1])
    upper_next[0] = send(first[0][:slots], lambda p, q: (p + 1, q))
    second[1] = after(second[1], lower_right[0])
    lower_right[1] = send(second[1], lambda p, q: (p - 1, q))
    upper_right = [value[:slots] for value in first]
    mirror = [value[slots:] for value in first]
    lower_next = second
    moved = send(jnp.concatenate(mirror), lambda p, q: (p, q + 1))
    mirror_next = [moved[:half], moved[half:]]
    stored_next = send(after(stored, first[0], second[0]), lambda p, q: (p, q + 1))

    def scalars(step):
        row = (p + step) % row_count
        start = (q + step) % col_count
        right = -row % col_count
        carry = (start + right - (q - p) % col_count) // col_count
        left_zero = start == 0
        right_zero = right == 0
        flip = q + step >= col_count
        left_swap = jnp.where(p % 2 == 0, start >= middle, start > middle)
        upper_swap = jnp.where(row % 2 == 0, q >= middle, q > middle)
        landed = (row - 1) % row_count
        sign = 1 - 2 * (landed % 2)
        amount = sign * (q - landed) % col_count
        near = landed + sign * amount + jnp.where(amount < middle, 0, col_count)
        lower_swap = ((near - q) % row_count // col_count + row // col_count) % 2
        return left_zero, flip, right_zero, carry, left_swap, upper_swap, lower_swap

    def packed(*values):
        return jnp.stack([jnp.asarray(value, jnp.int32) for value in values])

    def right_scalars(step, mirrored):
        left_zero, flip, right_zero, carry, left_swap, upper_swap, lower_swap = scalars(step)
        if mirrored:
            return packed(left_zero, flip, right_zero, carry + right_zero, left_swap, lower_swap)
        return packed(left_zero, flip, right_zero, carry + slots, left_swap, upper_swap)

    total = jnp.zeros((4 * slots, size, size), jnp.float32)
    total = add_products(total, False, right_scalars(0, False), *mirror, stored, *upper_right)
    total = add_products(total, True, right_scalars(1, True), *mirror_next, stored_next, *lower_next)
    total = add_products(total, False, right_scalars(1, False), *mirror_next, stored_next, *upper_next)
    total = add_products(total, True, right_scalars(0, True), *mirror, stored, *lower_right)
    return total.reshape(1, 1, 4 * slots, 1, size, size)


def solution(mesh):
    in_specs = (P(None, "row", None, "col", None, None), P(None, "row", None, "col"))
    out_specs = P(None, "row", None, "col", None, None)
    return jax.shard_map(
        per_device, mesh=mesh, in_specs=in_specs, out_specs=out_specs, check_vma=False
    )
```

```python
import jax
import jax.numpy as jnp
from jax import lax
from jax.experimental import pallas as pl
from jax.experimental.pallas import tpu as pltpu
from jax.sharding import PartitionSpec as P

MESH_AXES = ("row", "col")


def permute(value, row_count, col_count, source_of):
    pairs = []
    for p in range(row_count):
        for q in range(col_count):
            source_row, source_col = source_of(p, q)
            source = source_row % row_count * col_count + source_col % col_count
            pairs.append((source, p * col_count + q))
    return lax.ppermute(value, MESH_AXES, pairs)


def split(value):
    high = value.astype(jnp.bfloat16)
    return high, (value - high.astype(jnp.float32)).astype(jnp.bfloat16)


def band_kernel(mirrored, scalars, mirror_a, mirror_b, stored, right_a, right_b, total, out, left_high, left_low, tiles_high, tiles_low):
    half = mirror_a.shape[0]
    size = stored.shape[1]
    slots = stored.shape[0]
    left_zero = scalars[0]
    flip = scalars[1]
    right_zero = scalars[2]
    first = scalars[3]
    left_swap = scalars[4]
    right_swap = scalars[5]

    def put_left(slot, block):
        high, low = split(block)
        at = (pl.ds(slot // 2 * size, size), pl.ds(slot % 2 * size, size))
        left_high[at] = high
        left_low[at] = low

    for pair in range(half):
        pick = jnp.minimum(half - 1 - pair + left_zero, half - 1)
        block = jnp.where(left_swap == 0, mirror_a[pick], mirror_b[pick]).T
        if pair == 0:
            block = block * (1 - left_zero).astype(jnp.float32)
        put_left(2 * pair, block)
        put_left(2 * pair + 1, jnp.where(left_swap == 0, mirror_b[half - 1 - pair], mirror_a[half - 1 - pair]).T)
    for slot in range(slots):
        block = stored[slot]
        if slot == 0:
            block = block + block.T * left_zero.astype(jnp.float32)
        put_left(slots + slot, block)

    def right_block(layer, slot):
        swapped = (flip + right_swap + layer) % 2
        if mirrored:
            stored_slot = slots - 1 - slot
            swapped = swapped if stored_slot % 2 == 0 else 1 - swapped
            both = jnp.where(swapped == 0, right_a[stored_slot], right_b[stored_slot])
            if stored_slot == 0:
                both = both * (1 - right_zero).astype(jnp.float32)
            return both.T
        both = jnp.where(swapped == 0, right_a[slot], right_b[slot])
        if slot == 0:
            both = both + both.T * right_zero.astype(jnp.float32)
        return both

    zero = jnp.zeros((size, size), jnp.bfloat16)
    tile_count = slots // 2 + 1
    for tile in range(tile_count):
        for layer in range(2):
            for column in range(2):
                slot = 2 * tile + column - layer
                at = (tile, pl.ds(layer * size, size), pl.ds(column * size, size))
                if 0 <= slot < slots:
                    high, low = split(right_block(layer, slot))
                    tiles_high[at] = high
                    tiles_low[at] = low
                else:
                    tiles_high[at] = zero
                    tiles_low[at] = zero

    out[...] = total[...]
    left_pairs = left_high.shape[0] // size
    for tile in range(tile_count):
        high = tiles_high[tile]
        low = tiles_low[tile]
        for pair in range(left_pairs):
            rows = pl.ds(pair * size, size)
            part_high = left_high[rows, :]
            part = jnp.dot(part_high, high, preferred_element_type=jnp.float32)
            part = part + jnp.dot(part_high, low, preferred_element_type=jnp.float32)
            part = part + jnp.dot(left_low[rows, :], high, preferred_element_type=jnp.float32)
            at = 2 * (tile + pair) + first
            out[at] += part[:, :size]
            if tile < tile_count - 1:
                out[at + 1] += part[:, size:]


def add_products(total, mirrored, scalars, mirror_a, mirror_b, stored, right_a, right_b):
    slots, size, _ = stored.shape
    vmem = pl.BlockSpec(memory_space=pltpu.VMEM)

    def kernel(*refs):
        band_kernel(mirrored, *refs)

    return pl.pallas_call(
        kernel,
        out_shape=jax.ShapeDtypeStruct(total.shape, jnp.float32),
        in_specs=[pl.BlockSpec(memory_space=pltpu.SMEM)] + [vmem] * 6,
        out_specs=vmem,
        scratch_shapes=[
            pltpu.VMEM((slots * size, 2 * size), jnp.bfloat16),
            pltpu.VMEM((slots * size, 2 * size), jnp.bfloat16),
            pltpu.VMEM((slots // 2 + 1, 2 * size, 2 * size), jnp.bfloat16),
            pltpu.VMEM((slots // 2 + 1, 2 * size, 2 * size), jnp.bfloat16),
        ],
        compiler_params=pltpu.CompilerParams(vmem_limit_bytes=24 * 1024 * 1024),
        cost_estimate=pl.CostEstimate(flops=4 * slots * slots * size**3 * 3, bytes_accessed=4 * 1024 * 1024, transcendentals=0),
    )(scalars, mirror_a, mirror_b, stored, right_a, right_b, total)


def per_device(upper, mask):
    row_count = lax.axis_size("row")
    col_count = lax.axis_size("col")
    p = lax.axis_index("row")
    q = lax.axis_index("col")
    slots = upper.shape[2]
    size = upper.shape[4]
    half = slots // 2
    middle = col_count // 2

    def send(value, source_of):
        return permute(value, row_count, col_count, source_of)

    def after(value, *earlier):
        return lax.optimization_barrier((value, *earlier))[0]

    def shift_of(amount, order):
        near_is_same = amount < middle
        return amount if near_is_same == (order == 0) else amount + col_count

    def row_from(p, q):
        return p - q if (p + q) % 2 == 0 else p + q

    def signed(p, value):
        return value if p % 2 == 0 else -value

    def from_line(p, line, order):
        amount = shift_of(line, order)
        return (p + signed(p, amount), line)

    def sum_source(order):
        return lambda p, q: from_line(p, signed(p, q) % col_count, order)

    def col_source(order):
        return lambda p, q: from_line(p, signed(p, q - p) % col_count, order)

    present = mask.reshape(slots).astype(jnp.float32)
    stored = upper.reshape(slots, size, size) * present[:, None, None]
    by_parity = stored.reshape(half, 2, size, size)
    even, odd = by_parity[:, 0], by_parity[:, 1]
    target = -q % col_count
    near_is_other = jnp.where((p + target) % 2 == 0, target >= middle, target > middle)
    odd_first = (q != 0) != near_is_other
    for_left = jnp.concatenate([jnp.where(odd_first, odd, even), jnp.where(odd_first, even, odd)])

    via_upper = send(stored, lambda p, q: (p, -row_from(p, q)))
    via_left = send(for_left, lambda p, q: (p, row_from(p, q) - p))
    via_lower = send(after(stored, via_left), lambda p, q: (p, row_from(p, q) + 1))
    first = [None, None]
    second = [None, None]
    for order in (0, 1):
        half_of_left = via_left[order * half : (order + 1) * half]
        first[order] = send(jnp.concatenate([via_upper, half_of_left]), sum_source(order))
    for order in (0, 1):
        second[order] = send(via_lower, col_source(order))
    upper_next = [None, None]
    lower_right = [None, None]
    upper_next[1] = send(first[1][:slots], lambda p, q: (p + 1, q))
    lower_right[0] = send(second[0], lambda p, q: (p - 1, q))
    first[0] = after(first[0], upper_next[1])
    upper_next[0] = send(first[0][:slots], lambda p, q: (p + 1, q))
    second[1] = after(second[1], lower_right[0])
    lower_right[1] = send(second[1], lambda p, q: (p - 1, q))
    upper_right = [value[:slots] for value in first]
    mirror = [value[slots:] for value in first]
    lower_next = second
    moved = send(jnp.concatenate(mirror), lambda p, q: (p, q + 1))
    mirror_next = [moved[:half], moved[half:]]
    stored_next = send(after(stored, first[0], second[0]), lambda p, q: (p, q + 1))

    def scalars(step):
        row = (p + step) % row_count
        start = (q + step) % col_count
        right = -row % col_count
        carry = (start + right - (q - p) % col_count) // col_count
        left_zero = start == 0
        right_zero = right == 0
        flip = q + step >= col_count
        left_swap = jnp.where(p % 2 == 0, start >= middle, start > middle)
        upper_swap = jnp.where(row % 2 == 0, q >= middle, q > middle)
        landed = (row - 1) % row_count
        sign = 1 - 2 * (landed % 2)
        amount = sign * (q - landed) % col_count
        near = landed + sign * amount + jnp.where(amount < middle, 0, col_count)
        lower_swap = ((near - q) % row_count // col_count + row // col_count) % 2
        return left_zero, flip, right_zero, carry, left_swap, upper_swap, lower_swap

    def packed(*values):
        return jnp.stack([jnp.asarray(value, jnp.int32) for value in values])

    def right_scalars(step, mirrored):
        left_zero, flip, right_zero, carry, left_swap, upper_swap, lower_swap = scalars(step)
        if mirrored:
            return packed(left_zero, flip, right_zero, carry + right_zero, left_swap, lower_swap)
        return packed(left_zero, flip, right_zero, carry + slots, left_swap, upper_swap)

    total = jnp.zeros((4 * slots, size, size), jnp.float32)
    total = add_products(total, False, right_scalars(0, False), *mirror, stored, *upper_right)
    total = add_products(total, True, right_scalars(1, True), *mirror_next, stored_next, *lower_next)
    total = add_products(total, False, right_scalars(1, False), *mirror_next, stored_next, *upper_next)
    total = add_products(total, True, right_scalars(0, True), *mirror, stored, *lower_right)
    return total.reshape(1, 1, 4 * slots, 1, size, size)


def solution(mesh):
    in_specs = (P(None, "row", None, "col", None, None), P(None, "row", None, "col"))
    out_specs = P(None, "row", None, "col", None, None)
    return jax.shard_map(
        per_device, mesh=mesh, in_specs=in_specs, out_specs=out_specs, check_vma=False
    )
```
